32 devices in a mesh: lat: 4 (over y, x), lon: 8 (over z, core).
Axes of the slice: x: 2, y: 2, z: 4, core: 2. Of those that a mesh axis runs over, the one named last changes fastest.
Arguments:
- fields_in: bfloat16 [8, 256, 1024], P(None, 'lat', 'lon'), may hold values from -6 to 6
- hidden: bfloat16 [64, 256, 1024], P(None, 'lat', 'lon'), may hold values from -2.5 to 2.5
- cell_state: float32 [64, 256, 1024], P(None, 'lat', 'lon'), may hold values from -6 to 6
- analysis: bfloat16 [8, 256, 1024], P(None, 'lat', 'lon'), may hold values from -6 to 6, as said below
- gate_weight: bfloat16 [256, 648], replicated, may hold values from -0.25 to 0.25
- gate_bias: float32 [256], replicated, may hold values from -4 to 4
- out_weight: bfloat16 [8, 64], replicated, may hold values from -0.75 to 0.75
- relax_rates: float32 [8, 214], replicated, may hold values from 0.05 to 1
Outputs:
- fields_out: bfloat16 [8, 256, 1024], P(None, 'lat', 'lon')
- hidden_out: bfloat16 [64, 256, 1024], P(None, 'lat', 'lon')
- cell_out: float32 [64, 256, 1024], P(None, 'lat', 'lon')
The draws below stay inside these ranges and needn't reach their ends.
Inputs may be any that keep to these rules, and one draw needn't show every extreme that they name: analysis fields of order one.
All inputs are finite; a program needn't handle non-finite values.
Results may differ from the reference program's by a relative error of at most 0.009.
Values may be sent and summed in bfloat16 or wider, within the bound.
A program may use at most 448 MiB of HBM per device.

```python
import math
import jax
import jax.numpy as jnp
import numpy as np
from jax import lax

HID = 64
FIELDS = 8
TRUNC = 213
MODES = 224
KDEG = 214
LAT_DEV = 64
NLAT = 256
NLON = 1024
N_LAT = 4


def draw_analysis(key, part):
    noise_key, amp_key, north_key, zonal_key, shift_key = jax.random.split(jax.random.fold_in(key, 17), 5)
    lat_index = jnp.arange(NLAT, dtype=jnp.int32)
    lon_index = jnp.arange(NLON, dtype=jnp.int32)
    colatitude = (lat_index.astype(jnp.float32) + 0.5) * (math.pi / NLAT)
    amplitude = jax.random.uniform(amp_key, (FIELDS, 6), jnp.float32, -0.5, 0.5)
    zonal_wave = jax.random.randint(zonal_key, (6,), 1, 12)
    north_count = jax.random.randint(north_key, (6,), 1, 8)
    shifts = jax.random.uniform(shift_key, (6, 2), jnp.float32, -math.pi, math.pi)
    noise_part = 0.5 * jax.random.truncated_normal(noise_key, -4.0, 4.0, (FIELDS, NLAT, NLON), jnp.float32)
    summed = noise_part
    for wave_term in range(6):
        phases = (lon_index * zonal_wave[wave_term] % NLON).astype(jnp.float32) * (2.0 * math.pi / NLON)
        east_wave = jnp.cos(phases + shifts[wave_term, 0])
        north_wave = jnp.cos(colatitude * north_count[wave_term].astype(jnp.float32) + shifts[wave_term, 1])
        summed = summed + amplitude[:, wave_term][:, None, None] * north_wave[None, :, None] * east_wave[None, None, :]
    return summed.astype(jnp.bfloat16)


def block_scale(rng, shape, pieces, smallest, high):
    factor_of = 1.0
    for position, shards_of in pieces:
        draws = jax.random.uniform(jax.random.fold_in(jax.random.fold_in(rng, 6), position), (shards_of,), jnp.float32, smallest / len(pieces), high / len(pieces))
        factor_of = factor_of * jnp.repeat(jnp.exp(draws), shape[position] // shards_of).reshape((-1,) + (1,) * (len(shape) - 1 - position))
    return factor_of


def scatter_about(own_key, shape, scale, bound, cuts=(), held_as=jnp.bfloat16):
    result = jax.random.normal(own_key, shape, jnp.float32) * scale
    if len(cuts) > 0:
        result = block_scale(own_key, shape, cuts, -0.22, 0.18) * result
    return jnp.clip(result, min=-bound, max=bound).astype(held_as)


def setup_inputs(seed: int = 0) -> dict:
    key_of = jax.random.split(jax.random.key(seed), 9)
    return {
        "fields_in": scatter_about(key_of[0], (FIELDS, NLAT, NLON), 1.0, 6.0, ((1, 4), (2, 8))),
        "hidden": scatter_about(key_of[1], (HID, NLAT, NLON), 0.4, 2.5, ((1, 4), (2, 8))),
        "cell_state": scatter_about(key_of[2], (HID, NLAT, NLON), 1.0, 6.0, ((1, 4), (2, 8)), jnp.float32),
        "analysis": draw_analysis(jax.random.fold_in(key_of[8], 71), 0),
        "gate_weight": scatter_about(key_of[4], (4 * HID, 9 * (FIELDS + HID)), (9 * (FIELDS + HID)) ** -0.5, 0.25),
        "gate_bias": scatter_about(key_of[5], (4 * HID,), 1.0, 4.0, (), jnp.float32),
        "out_weight": scatter_about(key_of[6], (FIELDS, HID), HID ** -0.5, 0.75),
        "relax_rates": jnp.clip(jnp.exp(jax.random.uniform(key_of[7], (FIELDS, KDEG), jnp.float32, math.log(0.05), math.log(1.0))), 0.05, 1.0),
    }


precise = lax.Precision.HIGHEST

def recurrence_tables(mode_total, degree_count, truncation):
    order_grid = np.arange(mode_total) * 1.0
    ratios = np.ones(mode_total)
    ratios[1:] = (2.0 * order_grid[1:] + 1.0) / (2.0 * order_grid[1:])
    diag_log = 0.5 * np.log(0.5) + np.cumsum(0.5 * np.log(ratios))
    first_factor = np.sqrt(2.0 * order_grid + 3.0)
    degree_grid = order_grid[None, :] + np.arange(degree_count)[:, None] * 1.0
    lower_sq = np.maximum(degree_grid ** 2 - order_grid[None, :] ** 2, 1.0)
    prior_sq = np.maximum((degree_grid - 1.0) ** 2 - order_grid[None, :] ** 2, 0.0)
    alpha_rec = np.sqrt((4.0 * degree_grid ** 2 - 1.0) / lower_sq)
    beta_rec = np.sqrt(prior_sq / np.maximum(4.0 * (degree_grid - 1.0) ** 2 - 1.0, 1.0))
    retain = np.where(degree_grid <= truncation, 1.0, 0.0)
    return (diag_log, first_factor, alpha_rec, beta_rec, retain)

def legendre(mode_first, mode_count, row_first, row_count, lat_total):
    diag_log, first_factor, alpha_rec, beta_rec, retain = recurrence_tables(MODES, KDEG, TRUNC)

    def window(values, axis_pos):
        return lax.dynamic_slice_in_dim(jnp.asarray(values, dtype=jnp.float32), mode_first, mode_count, axis_pos)
    row_index = row_first + jnp.arange(row_count, dtype=jnp.int32)
    latitude = (row_index.astype(jnp.float32) + 0.5) * (math.pi / lat_total) - 0.5 * math.pi
    lat_sine = jnp.sin(latitude)
    lat_cosine = jnp.cos(latitude)
    weights = lat_cosine * (math.pi / lat_total)
    orders = (mode_first + jnp.arange(mode_count, dtype=jnp.int32)).astype(jnp.float32)
    diagonal = jnp.exp(window(diag_log, 0)[:, None] + orders[:, None] * jnp.log(lat_cosine)[None, :])
    second = window(first_factor, 0)[:, None] * lat_sine[None, :] * diagonal

    def advance(carry, factors):
        previous, current = carry
        upcoming = factors[0][:, None] * (lat_sine[None, :] * current - factors[1][:, None] * previous)
        return ((current, upcoming), upcoming)
    carry_out, remaining = lax.scan(advance, (diagonal, second), (window(alpha_rec, 1)[2:], window(beta_rec, 1)[2:]), unroll=True)
    values = jnp.concatenate([diagonal[None], second[None], remaining], axis=0)
    return (values * window(retain, 1)[:, :, None], weights)

def fourier_tables(col_first, col_count, lon_total):
    columns = (col_first + jnp.arange(col_count, dtype=jnp.int32)).astype(jnp.int32)
    orders = jnp.arange(MODES, dtype=jnp.int32)
    phases = columns[:, None] * orders[None, :] % lon_total
    angles = phases.astype(jnp.float32) * (2.0 * math.pi / lon_total)
    retain = (orders <= TRUNC).astype(jnp.float32)
    forward = jnp.stack([jnp.cos(angles) * retain, jnp.sin(angles) * retain], axis=1)
    scales = jnp.where(orders == 0, 1.0, 2.0).astype(jnp.float32) / lon_total
    inverse = forward * scales[None, None, :]
    return (forward.reshape(col_count, 2 * MODES), inverse.reshape(col_count, 2 * MODES))

def lstm_tile(padded, cell_state, fields_in, gate_weight, gate_bias, out_weight):
    lat_rows = cell_state.shape[1]
    lon_cols = cell_state.shape[2]
    channels = padded.shape[0]
    views = []
    for row_shift in range(3):
        for col_shift in range(3):
            views.append(padded[:, row_shift:row_shift + lat_rows, col_shift:col_shift + lon_cols].reshape(channels, -1))
    patches = jnp.concatenate(views, axis=0)
    gate_sums = jnp.dot(gate_weight, patches, preferred_element_type=jnp.float32)
    gate_sums = gate_sums.reshape(4, -1, lat_rows, lon_cols) + gate_bias.reshape(4, -1, 1, 1)
    input_gate = jax.nn.sigmoid(gate_sums[0])
    forget = jax.nn.sigmoid(gate_sums[1])
    candidate = jnp.tanh(gate_sums[2])
    output = jax.nn.sigmoid(gate_sums[3])
    cell_out = forget * cell_state + input_gate * candidate
    hidden_out = (output * jnp.tanh(cell_out)).astype(jnp.bfloat16)
    increment = jnp.dot(out_weight, hidden_out.reshape(hidden_out.shape[0], -1), preferred_element_type=jnp.float32)
    predicted = fields_in.astype(jnp.float32) + increment.reshape(fields_in.shape)
    return (cell_out, hidden_out, predicted)

def reference(fields_in, hidden, cell_state, analysis, gate_weight, gate_bias, out_weight, relax_rates):
    stacked = jnp.concatenate([fields_in, hidden], axis=0)
    padded = jnp.pad(stacked, ((0, 0), (0, 0), (1, 1)), mode='wrap')
    padded = jnp.pad(padded, ((0, 0), (1, 1), (0, 0)))

    def one_band(band_index):
        first_row = (band_index * LAT_DEV).astype(jnp.int32)
        band_slab = lax.dynamic_slice_in_dim(padded, first_row, LAT_DEV + 2, 1)
        cell_slab = lax.dynamic_slice_in_dim(cell_state, first_row, LAT_DEV, 1)
        field_slab = lax.dynamic_slice_in_dim(fields_in, first_row, LAT_DEV, 1)
        return lstm_tile(band_slab, cell_slab, field_slab, gate_weight, gate_bias, out_weight)
    cell_bands, hidden_bands, predicted_bands = lax.map(one_band, jnp.arange(N_LAT, dtype=jnp.int32))

    def unband(values):
        return jnp.moveaxis(values, 0, 1).reshape(values.shape[1], NLAT, NLON)
    cell_out = unband(cell_bands)
    hidden_out = unband(hidden_bands)
    predicted = unband(predicted_bands)
    mismatch = analysis.astype(jnp.float32) - fields_in.astype(jnp.float32)
    forward, inverse = fourier_tables(0, NLON, NLON)
    fourier = jnp.einsum('flx,xq->flq', mismatch, forward, precision=precise).reshape(FIELDS, NLAT, 2, MODES)
    basis, weights = legendre(0, MODES, 0, NLAT, NLAT)
    spectrum = jnp.einsum('flpm,kml->fpmk', fourier, basis * weights[None, None, :], precision=precise)
    degree = jnp.clip(jnp.arange(MODES, dtype=jnp.int32)[:, None] + jnp.arange(KDEG, dtype=jnp.int32)[None, :], 0, KDEG - 1)
    nudge_rates = jnp.take(relax_rates, degree, axis=1)
    regridded = jnp.einsum('fpmk,kml->flpm', spectrum * nudge_rates[:, None], basis, precision=precise)
    correction = jnp.einsum('flq,xq->flx', regridded.reshape(FIELDS, NLAT, 2 * MODES), inverse, precision=precise)
    fields_out = (predicted + correction).astype(jnp.bfloat16)
    return (fields_out, hidden_out, cell_out)
```

```python
import functools
import math

import jax
import jax.numpy as jnp
import numpy as np
from jax import lax
from jax.experimental import pallas as pl
from jax.experimental.pallas import tpu as pltpu
from jax.sharding import PartitionSpec as P

FIELDS = 8
TRUNC = 213
MODES = 224
KDEG = 214
CH = 80
QP = 16
KP = 256
MESH = pl.DeviceIdType.MESH
F32 = jnp.float32
BF16 = jnp.bfloat16


def legendre_table(lat_total, owners, share):
    order = np.arange(MODES) * 1.0
    ratios = np.ones(MODES)
    ratios[1:] = (2.0 * order[1:] + 1.0) / (2.0 * order[1:])
    diag_log = 0.5 * np.log(0.5) + np.cumsum(0.5 * np.log(ratios))
    phi = -0.5 * np.pi + (np.arange(lat_total) + 0.5) * np.pi / lat_total
    sine, cosine = np.sin(phi), np.cos(phi)
    table = np.zeros((KDEG, MODES, lat_total))
    table[0] = np.exp(diag_log[:, None] + order[:, None] * np.log(cosine)[None, :])
    table[1] = np.sqrt(2.0 * order + 3.0)[:, None] * sine[None, :] * table[0]
    for k in range(2, KDEG):
        n = order + k
        alpha = np.sqrt((4.0 * n**2 - 1.0) / (n**2 - order**2))
        beta = np.sqrt(((n - 1.0) ** 2 - order**2) / (4.0 * (n - 1.0) ** 2 - 1.0))
        table[k] = alpha[:, None] * (sine[None, :] * table[k - 1] - beta[:, None] * table[k - 2])
    degree = order[None, :] + np.arange(KDEG)[:, None]
    table *= (degree <= TRUNC)[:, :, None]
    full = np.zeros((owners * share, KP, lat_total), dtype=BF16)
    full[:MODES, :KDEG] = table.transpose(1, 0, 2).astype(np.float32).astype(BF16)
    return full.reshape(owners, share * KP, lat_total)


def trig_table(lon_total, owners, share):
    m = np.arange(owners * share)
    phase = (m[:, None] * np.arange(lon_total)[None, :]) % lon_total
    angle = phase * (2.0 * np.pi / lon_total)
    both = np.stack([np.cos(angle), np.sin(angle)], axis=1) * (m <= TRUNC)[:, None, None]
    full = np.zeros((owners, QP, lon_total))
    full[:, : 2 * share] = both.reshape(owners, 2 * share, lon_total)
    return full.reshape(owners * QP, lon_total).astype(np.float32).astype(BF16)


def kernel(
    lats, lons, share, rows, cols,
    fields_ref, hidden_ref, cell_ref, analysis_ref, gw_ref, bias_ref, ow_ref, relax_ref,
    weights_ref, trig_hbm, leg_hbm,
    fields_out, hidden_out, cell_out,
    send1, r1, fh, slab, cols_out, halo, cols_in, fsend, r2, xbuf, ysend, r3, csend, r4,
    gate_w, pred, hid, trig, leg, cell,
    load_sem, s1, v1, s2, v2, s3, v3, s4, v4, sh, vh,
):
    a, b = lax.axis_index("lat"), lax.axis_index("lon")
    owners = lats * lons
    me = a * lons + b
    piece = FIELDS * rows // lons
    per_field = rows // piece
    packs = 128 // piece
    group = a * per_field + lax.rem(b, per_field)
    own_row = pl.multiple_of(lax.rem(group, packs) * piece, piece)
    lon_total = lons * cols

    load_trig = pltpu.make_async_copy(trig_hbm, trig, load_sem.at[0])
    load_leg = pltpu.make_async_copy(leg_hbm.at[me], leg, load_sem.at[1])
    load_cell = pltpu.make_async_copy(cell_ref, cell, load_sem.at[2])
    load_trig.start()
    load_leg.start()
    load_cell.start()

    r1[...] = jnp.zeros_like(r1)
    barrier = pltpu.get_barrier_semaphore()

    def greet(i, _):
        peer = lax.rem(me + i, owners)
        pl.semaphore_signal(
            barrier, inc=1, device_id=(peer // lons, lax.rem(peer, lons)), device_id_type=MESH
        )
        return 0

    lax.fori_loop(1, owners, greet, 0)

    send1[...] = (analysis_ref[...].astype(F32) - fields_ref[...].astype(F32)).astype(BF16)
    pl.semaphore_wait(barrier, owners - 1)

    def lon_copy(i, src, dst, ssem, rsem):
        return pltpu.make_async_remote_copy(
            src_ref=src, dst_ref=dst, send_sem=ssem.at[i], recv_sem=rsem.at[i],
            device_id=(a, lax.rem(b + i, lons)), device_id_type=MESH,
        )

    def first(i):
        peer = lax.rem(b + i, lons)
        src = send1.at[pl.ds(pl.multiple_of(peer * piece, piece), piece)]
        return lon_copy(i, src, r1.at[b, pl.ds(own_row, piece)], s1, v1)

    def loop(start, stop, fn):
        def body(i, _):
            fn(i)
            return 0
        lax.fori_loop(start, stop, body, 0)

    loop(1, lons, lambda i: first(i).start())
    r1[b, pl.ds(own_row, piece), :] = send1[pl.ds(pl.multiple_of(b * piece, piece), piece), :]

    fh[0 : FIELDS * rows, :] = fields_ref[...].astype(F32)

    def widen(c):
        at = pl.multiple_of(c * 512, 512)
        fh[pl.ds(pl.multiple_of(at + FIELDS * rows, 512), 512), :] = hidden_ref[
            pl.ds(at, 512), :
        ].astype(F32)

    loop(0, hidden_ref.shape[0] // 512, widen)
    lane = lax.broadcasted_iota(jnp.int32, (CH, cols), 1)
    ones = jnp.ones((8, cols), F32)

    def turn(r, carry):
        west, east = carry
        t = jnp.concatenate([fh[pl.ds(r, CH - 8, stride=rows), :], ones], axis=0)
        slab[r + 1, CH : 2 * CH, :] = t.astype(BF16)
        west = jnp.where(lane == r, jnp.broadcast_to(t[:, 0:1], (CH, cols)), west)
        east = jnp.where(lane == r, jnp.broadcast_to(t[:, cols - 1 : cols], (CH, cols)), east)
        return west, east

    zero = jnp.zeros((CH, cols), F32)
    west, east = lax.fori_loop(0, rows, turn, (zero, zero))
    cols_out[0] = west.astype(BF16)
    cols_out[1] = east.astype(BF16)

    left, right = lax.rem(b + lons - 1, lons), lax.rem(b + 1, lons)

    def rim(slot, src, dst, la, lo):
        return pltpu.make_async_remote_copy(
            src_ref=src, dst_ref=dst, send_sem=sh.at[slot], recv_sem=vh.at[slot],
            device_id=(la, lo), device_id_type=MESH,
        )

    north, south = jnp.maximum(a - 1, 0), jnp.minimum(a + 1, lats - 1)
    to_south = [
        rim(0, slab.at[rows, pl.ds(CH, CH)], halo.at[0], south, b),
        rim(1, cols_out.at[1], cols_in.at[0, 0], south, right),
        rim(2, cols_out.at[0], cols_in.at[1, 0], south, left),
    ]
    to_north = [
        rim(3, slab.at[1, pl.ds(CH, CH)], halo.at[1], north, b),
        rim(4, cols_out.at[1], cols_in.at[0, 2], north, right),
        rim(5, cols_out.at[0], cols_in.at[1, 2], north, left),
    ]
    level = [
        rim(6, cols_out.at[1], cols_in.at[0, 1], a, right),
        rim(7, cols_out.at[0], cols_in.at[1, 1], a, left),
    ]
    for copy in level:
        copy.start()

    @pl.when(a < lats - 1)
    def _():
        for copy in to_south:
            copy.start()

    @pl.when(a > 0)
    def _():
        for copy in to_north:
            copy.start()

    load_trig.wait()
    loop(1, lons, lambda i: first(i).wait())
    lat_weight = weights_ref[pl.ds(group // packs, 1), :]
    tall = min(512, owners * QP)

    def zonal(c):
        at = pl.multiple_of(c * tall, tall)
        total = jnp.zeros((tall, 128), F32)
        for x in range(lons):
            total += lax.dot_general(
                trig[pl.ds(at, tall), x * cols : (x + 1) * cols], r1[x],
                (((1,), (1,)), ((), ())), preferred_element_type=F32,
            )
        fsend[pl.ds(at, tall), :] = (total * lat_weight).astype(BF16)

    loop(0, owners * QP // tall, zonal)

    def own_block(ref, d):
        return ref.at[pl.ds(pl.multiple_of(d * QP, QP), QP)]

    def second(i):
        peer = lax.rem(me + i, owners)
        return pltpu.make_async_remote_copy(
            src_ref=own_block(fsend, peer), dst_ref=own_block(r2, me),
            send_sem=s2.at[i], recv_sem=v2.at[i],
            device_id=(peer // lons, lax.rem(peer, lons)), device_id_type=MESH,
        )

    loop(1, owners, lambda i: second(i).start())
    mine = pl.ds(pl.multiple_of(me * QP, QP), QP)
    r2[mine, :] = fsend[mine, :]

    wide = 9 * CH
    spot = lax.broadcasted_iota(jnp.int32, (1, wide), 1)
    tap = spot // CH
    within = spot - tap * CH
    source = jnp.where(within < CH - 8, tap * (CH - 8) + within, -1)
    pick = lax.broadcasted_iota(jnp.int32, (gw_ref.shape[1], wide), 0) == source
    spread = jnp.dot(
        gw_ref[...], jnp.where(pick, 1.0, 0.0).astype(BF16), preferred_element_type=F32
    )
    bias = jnp.transpose(jnp.broadcast_to(bias_ref[...], (128, 256)))[:, 0:1]
    high = bias.astype(BF16).astype(F32)
    middle = (bias - high).astype(BF16).astype(F32)
    low = bias - high - middle
    base = 4 * CH + CH - 8
    spread += jnp.where(spot == base, high, 0.0)
    spread += jnp.where(spot == base + 1, middle, 0.0)
    spread += jnp.where(spot == base + 2, low, 0.0)
    gate_row = lax.broadcasted_iota(jnp.int32, (256, 1), 0) // 64
    gate_w[...] = (spread * jnp.where(gate_row == 2, 1.0, 0.5)).astype(BF16)

    for copy in level:
        copy.wait()

    @pl.when(a < lats - 1)
    def _():
        for copy in to_south:
            copy.wait_send()
        for copy in to_north:
            copy.wait_recv()

    @pl.when(a > 0)
    def _():
        for copy in to_north:
            copy.wait_send()
        for copy in to_south:
            copy.wait_recv()

    @pl.when(a == 0)
    def _():
        halo[0] = jnp.zeros((CH, cols), BF16)
        cols_in[0, 0] = jnp.zeros((CH, cols), BF16)
        cols_in[1, 0] = jnp.zeros((CH, cols), BF16)

    @pl.when(a == lats - 1)
    def _():
        halo[1] = jnp.zeros((CH, cols), BF16)
        cols_in[0, 2] = jnp.zeros((CH, cols), BF16)
        cols_in[1, 2] = jnp.zeros((CH, cols), BF16)

    def shifted(t, from_west, from_east, row, at):
        before = jnp.where(lane == 0, pltpu.roll(from_west, lax.rem(cols - row, cols), 1), pltpu.roll(t, 1, 1))
        after = jnp.where(
            lane == cols - 1, pltpu.roll(from_east, cols - 1 - row, 1), pltpu.roll(t, cols - 1, 1)
        )
        slab[at, 0:CH, :] = before.astype(BF16)
        slab[at, 2 * CH : 3 * CH, :] = after.astype(BF16)

    def shift_row(r):
        t = slab[r + 1, CH : 2 * CH, :].astype(F32)
        shifted(t, cols_in[0, 1].astype(F32), cols_in[1, 1].astype(F32), r, r + 1)

    loop(0, rows, shift_row)
    slab[0, CH : 2 * CH, :] = halo[0]
    slab[rows + 1, CH : 2 * CH, :] = halo[1]
    shifted(halo[0].astype(F32), cols_in[0, 0].astype(F32), cols_in[1, 0].astype(F32), rows - 1, 0)
    shifted(halo[1].astype(F32), cols_in[0, 2].astype(F32), cols_in[1, 2].astype(F32), 0, rows + 1)

    load_leg.wait()
    loop(1, owners, lambda i: second(i).wait())
    tiles = lats * rows // 128
    for f in range(FIELDS):
        for t in range(tiles):
            total = jnp.zeros((QP, 128), F32)
            for s in range(packs):
                g = t * packs + s
                d = (g // per_field) * lons + f * per_field + g % per_field
                total += r2[d * QP : (d + 1) * QP, :].astype(F32)
            xbuf[f * QP : (f + 1) * QP, t * 128 : (t + 1) * 128] = total.astype(BF16)
    x = xbuf[...]
    y = jnp.zeros((FIELDS * QP, lats * rows), F32)
    q_mode = lax.rem(lax.broadcasted_iota(jnp.int32, (FIELDS * QP, KP), 0), QP) // 2
    m_first = me * share
    rates = pltpu.roll(relax_ref[...], lax.rem(512 - m_first, 512), 1)
    for i in range(share):
        basis = leg[i * KP : (i + 1) * KP, :]
        s = lax.dot_general(x, basis, (((1,), (1,)), ((), ())), preferred_element_type=F32)
        rate = (rates if i == 0 else pltpu.roll(rates, 512 - i, 1))[:, :KP]
        rate = rate * jnp.where(m_first + i == 0, 1.0 / lon_total, 2.0 / lon_total)
        rate = jnp.broadcast_to(rate[:, None, :], (FIELDS, QP, KP)).reshape(FIELDS * QP, KP)
        s = jnp.where(q_mode == i, s * rate, 0.0).astype(BF16)
        y += jnp.dot(s, basis, preferred_element_type=F32)
    y = y.astype(BF16)
    for t in range(tiles):
        ysend[t] = y[:, t * 128 : (t + 1) * 128]

    def reply(d):
        la, lo = d // lons, lax.rem(d, lons)
        t = (la * per_field + lax.rem(lo, per_field)) // packs
        return t, pl.ds(pl.multiple_of((lo // per_field) * QP, QP), QP)

    def third(i):
        peer = lax.rem(me + i, owners)
        t, at = reply(peer)
        return pltpu.make_async_remote_copy(
            src_ref=ysend.at[t, at], dst_ref=own_block(r3, me),
            send_sem=s3.at[i], recv_sem=v3.at[i],
            device_id=(peer // lons, lax.rem(peer, lons)), device_id_type=MESH,
        )

    loop(1, owners, lambda i: third(i).start())
    t_own, at_own = reply(me)
    r3[mine, :] = ysend[t_own, at_own, :]

    load_cell.wait()

    def pair(i):
        r = 2 * i
        patches = jnp.concatenate(
            [slab[pl.ds(r, 3)].reshape(wide, cols), slab[pl.ds(r + 1, 3)].reshape(wide, cols)], axis=1
        )
        g = jnp.tanh(jnp.dot(gate_w[...], patches, preferred_element_type=F32))
        old = jnp.concatenate(
            [cell[pl.ds(r, 64, stride=rows), :], cell[pl.ds(r + 1, 64, stride=rows), :]], axis=1
        )
        new = (0.5 * g[64:128] + 0.5) * old + (0.5 * g[0:64] + 0.5) * g[128:192]
        h = (0.5 * g[192:256] + 0.5) * jnp.tanh(new)
        cell_out[pl.ds(r, 64, stride=rows), :] = new[:, :cols]
        cell_out[pl.ds(r + 1, 64, stride=rows), :] = new[:, cols:]
        hid[pl.ds(r, 64, stride=rows), :] = h[:, :cols]
        hid[pl.ds(r + 1, 64, stride=rows), :] = h[:, cols:]
        inc = jnp.dot(ow_ref[...], h.astype(BF16), preferred_element_type=F32)
        pred[pl.ds(r, FIELDS, stride=rows), :] = inc[:, :cols]
        pred[pl.ds(r + 1, FIELDS, stride=rows), :] = inc[:, cols:]

    loop(0, rows // 4, pair)

    loop(1, owners, lambda i: third(i).wait())
    for c in range(lons):
        csend[c] = lax.dot_general(
            r3[...], trig[:, c * cols : (c + 1) * cols], (((0,), (0,)), ((), ())),
            preferred_element_type=F32,
        ).astype(BF16)
    spot4 = pl.ds(pl.multiple_of(b * piece, piece), piece)

    def fourth(i):
        peer = lax.rem(b + i, lons)
        return lon_copy(i, csend.at[peer, pl.ds(own_row, piece)], r4.at[spot4], s4, v4)

    loop(1, lons, lambda i: fourth(i).start())
    r4[spot4, :] = csend[b, pl.ds(own_row, piece), :]

    loop(rows // 4, rows // 2, pair)

    def narrow(c):
        at = pl.ds(pl.multiple_of(c * 512, 512), 512)
        hidden_out[at, :] = hid[at, :].astype(BF16)

    loop(0, hidden_ref.shape[0] // 512, narrow)
    loop(1, lons, lambda i: fourth(i).wait())
    fields_out[...] = (
        fields_ref[...].astype(F32) + pred[...] + r4[...].astype(F32)
    ).astype(BF16)


def local(lats, lons, leg, trig, share, fields_in, hidden, cell_state, analysis, gate_weight, gate_bias, out_weight, relax_rates):
    hid, rows, cols = cell_state.shape
    owners = lats * lons
    lat_total = lats * rows
    piece = FIELDS * rows // lons
    phi = -0.5 * np.pi + (np.arange(lat_total) + 0.5) * np.pi / lat_total
    weights = (np.cos(phi) * np.pi / lat_total).astype(np.float32).reshape(-1, 128)
    vm = pl.BlockSpec(memory_space=pltpu.VMEM)
    hbm = pl.BlockSpec(memory_space=pl.ANY)
    n_rows = FIELDS * rows
    dma = pltpu.SemaphoreType.DMA
    relax = jnp.pad(relax_rates, ((0, 0), (0, 512 - KDEG)))
    out = pl.pallas_call(
        functools.partial(kernel, lats, lons, share, rows, cols),
        out_shape=(
            jax.ShapeDtypeStruct((n_rows, cols), BF16),
            jax.ShapeDtypeStruct((hid * rows, cols), BF16),
            jax.ShapeDtypeStruct((hid * rows, cols), F32),
        ),
        in_specs=[vm, vm, hbm, vm, vm, vm, vm, vm, vm, hbm, hbm],
        out_specs=(vm, vm, vm),
        scratch_shapes=[
            pltpu.VMEM((n_rows, cols), BF16),
            pltpu.VMEM((lons, 128, cols), BF16),
            pltpu.VMEM(((hid + FIELDS) * rows, cols), F32),
            pltpu.VMEM((rows + 2, 3 * CH, cols), BF16),
            pltpu.VMEM((2, CH, cols), BF16),
            pltpu.VMEM((2, CH, cols), BF16),
            pltpu.VMEM((2, 3, CH, cols), BF16),
            pltpu.VMEM((owners * QP, 128), BF16),
            pltpu.VMEM((owners * QP, 128), BF16),
            pltpu.VMEM((FIELDS * QP, lat_total), BF16),
            pltpu.VMEM((lat_total // 128, FIELDS * QP, 128), BF16),
            pltpu.VMEM((owners * QP, 128), BF16),
            pltpu.VMEM((lons, 128, cols), BF16),
            pltpu.VMEM((n_rows, cols), BF16),
            pltpu.VMEM((4 * hid, 9 * CH), BF16),
            pltpu.VMEM((n_rows, cols), F32),
            pltpu.VMEM((hid * rows, cols), F32),
            pltpu.VMEM(trig.shape, BF16),
            pltpu.VMEM(leg.shape[1:], BF16),
            pltpu.VMEM((hid * rows, cols), F32),
            dma((3,)),
            dma((lons,)), dma((lons,)), dma((owners,)), dma((owners,)),
            dma((owners,)), dma((owners,)), dma((lons,)), dma((lons,)),
            dma((8,)), dma((8,)),
        ],
        compiler_params=pltpu.CompilerParams(
            collective_id=0, has_side_effects=True, vmem_limit_bytes=56 * 1024 * 1024
        ),
    )(
        fields_in.reshape(n_rows, cols), hidden.reshape(hid * rows, cols),
        cell_state.reshape(hid * rows, cols), analysis.reshape(n_rows, cols),
        gate_weight, gate_bias.reshape(1, -1), out_weight, relax, jnp.asarray(weights),
        jnp.asarray(trig), jnp.asarray(leg),
    )
    return (
        out[0].reshape(fields_in.shape), out[1].reshape(hidden.shape), out[2].reshape(cell_state.shape)
    )


def solution(mesh):
    lats, lons = mesh.shape["lat"], mesh.shape["lon"]
    owners = lats * lons
    share = -(-MODES // owners)

    def whole(*args):
        lat_total, lon_total = args[2].shape[1:]
        leg = legendre_table(lat_total, owners, share)
        trig = trig_table(lon_total, owners, share)
        grid = P(None, "lat", "lon")
        return jax.shard_map(
            functools.partial(local, lats, lons, leg, trig, share),
            mesh=mesh,
            in_specs=(grid, grid, grid, grid, P(), P(), P(), P()),
            out_specs=(grid, grid, grid),
            check_vma=False,
        )(*args)

    return whole
```

```python
import functools
import math

import jax
import jax.numpy as jnp
import numpy as np
from jax import lax
from jax.experimental import pallas as pl
from jax.experimental.pallas import tpu as pltpu
from jax.sharding import PartitionSpec as P

FIELDS = 8
TRUNC = 213
MODES = 224
KDEG = 214
CH = 80
MESH = pl.DeviceIdType.MESH
F32 = jnp.float32
BF16 = jnp.bfloat16


def legendre_table(lat_total, members):
    order = np.arange(MODES) * 1.0
    ratios = np.ones(MODES)
    ratios[1:] = (2.0 * order[1:] + 1.0) / (2.0 * order[1:])
    diag_log = 0.5 * np.log(0.5) + np.cumsum(0.5 * np.log(ratios))
    phi = -0.5 * np.pi + (np.arange(lat_total) + 0.5) * np.pi / lat_total
    sine, cosine = np.sin(phi), np.cos(phi)
    table = np.zeros((KDEG, MODES, lat_total))
    table[0] = np.exp(diag_log[:, None] + order[:, None] * np.log(cosine)[None, :])
    table[1] = np.sqrt(2.0 * order + 3.0)[:, None] * sine[None, :] * table[0]
    for k in range(2, KDEG):
        n = order + k
        alpha = np.sqrt((4.0 * n**2 - 1.0) / (n**2 - order**2))
        beta = np.sqrt(((n - 1.0) ** 2 - order**2) / (4.0 * (n - 1.0) ** 2 - 1.0))
        table[k] = alpha[:, None] * (sine[None, :] * table[k - 1] - beta[:, None] * table[k - 2])
    degree = order[None, :] + np.arange(KDEG)[:, None]
    table *= (degree <= TRUNC)[:, :, None]
    offsets = degree_offsets(members)
    full = np.zeros((members, offsets[-1], lat_total))
    for member in range(members):
        for i, m in enumerate(range(member, MODES, members)):
            count = min(offsets[i + 1] - offsets[i], KDEG)
            full[member, offsets[i] : offsets[i] + count] = table[:count, m]
    return full.astype(np.float32).astype(BF16)


def degree_offsets(members):
    offsets = [0]
    for i in range(-(-MODES // members)):
        offsets.append(offsets[-1] + (256 if KDEG - members * i > 128 else 128))
    return offsets


def block_rows(members):
    return -(-2 * -(-MODES // members) // 16) * 16


def trig_table(lon_total, members):
    m = np.arange(-(-MODES // members) * members)
    phase = (m[:, None] * np.arange(lon_total)[None, :]) % lon_total
    angle = phase * (2.0 * np.pi / lon_total)
    both = np.stack([np.cos(angle), np.sin(angle)], axis=1) * (m <= TRUNC)[:, None, None]
    full = np.zeros((members, block_rows(members), lon_total))
    for member in range(members):
        part = both[member::members].reshape(-1, lon_total)
        full[member, : part.shape[0]] = part
    return full.reshape(-1, lon_total).astype(np.float32).astype(BF16)


def loop(start, stop, fn):
    def body(i, _):
        fn(i)
        return 0

    lax.fori_loop(start, stop, body, 0)


def kernel(
    lats, lons, rows, cols,
    fields_ref, hidden_ref, cell_ref, analysis_ref, gw_ref, bias_ref, ow_ref, relax_ref,
    weights_ref, trig_hbm, leg_hbm,
    fields_out, hidden_out, cell_out,
    send1, r1, fh, slab, cols_out, halo, cols_in, fsend, r2, ysend, r3, turned, csend, r4, rates,
    gate_w, pred, hid, trig, leg, cell,
    load_sem, s1, v1, s2, v2, s3, v3, s4, v4, sh, vh,
):
    a, b = lax.axis_index("lat"), lax.axis_index("lon")
    piece = FIELDS * rows // lons
    per_field = rows // piece
    packs = 128 // piece
    group = a * per_field + lax.rem(b, per_field)
    members = lats * per_field
    block = block_rows(members)
    own_row = pl.multiple_of(lax.rem(group, packs) * piece, piece)
    lon_total = lons * cols

    load_trig = pltpu.make_async_copy(trig_hbm, trig, load_sem.at[0])
    load_leg = pltpu.make_async_copy(leg_hbm.at[group], leg, load_sem.at[1])
    load_cell = pltpu.make_async_copy(cell_ref, cell, load_sem.at[2])
    load_trig.start()
    load_leg.start()
    load_cell.start()

    r1[...] = jnp.zeros_like(r1)
    barrier = pltpu.get_barrier_semaphore()

    def member_device(member):
        return member // per_field, b - lax.rem(b, per_field) + lax.rem(member, per_field)

    def hello(la, lo):
        pl.semaphore_signal(barrier, inc=1, device_id=(la, lo), device_id_type=MESH)

    loop(1, lons, lambda i: hello(a, lax.rem(b + i, lons)))
    loop(1, members, lambda i: hello(*member_device(lax.rem(group + i, members))))
    left, right = lax.rem(b + lons - 1, lons), lax.rem(b + 1, lons)
    north, south = jnp.maximum(a - 1, 0), jnp.minimum(a + 1, lats - 1)

    @pl.when(a > 0)
    def _():
        hello(north, left)
        hello(north, right)

    @pl.when(a < lats - 1)
    def _():
        hello(south, left)
        hello(south, right)

    send1[...] = (analysis_ref[...].astype(F32) - fields_ref[...].astype(F32)).astype(BF16)
    greeted = lons + members - 2
    greeted += 2 * (a > 0).astype(jnp.int32) + 2 * (a < lats - 1).astype(jnp.int32)
    pl.semaphore_wait(barrier, greeted)

    def lon_copy(i, src, dst, ssem, rsem):
        return pltpu.make_async_remote_copy(
            src_ref=src, dst_ref=dst, send_sem=ssem.at[i], recv_sem=rsem.at[i],
            device_id=(a, lax.rem(b + i, lons)), device_id_type=MESH,
        )

    def first(i):
        peer = lax.rem(b + i, lons)
        src = send1.at[pl.ds(pl.multiple_of(peer * piece, piece), piece)]
        return lon_copy(i, src, r1.at[b, pl.ds(own_row, piece)], s1, v1)

    loop(1, lons, lambda i: first(i).start())
    r1[b, pl.ds(own_row, piece), :] = send1[pl.ds(pl.multiple_of(b * piece, piece), piece), :]

    fh[0 : FIELDS * rows, :] = fields_ref[...].astype(F32)

    def widen(c):
        at = pl.multiple_of(c * 512, 512)
        fh[pl.ds(pl.multiple_of(at + FIELDS * rows, 512), 512), :] = hidden_ref[
            pl.ds(at, 512), :
        ].astype(F32)

    loop(0, hidden_ref.shape[0] // 512, widen)
    lane = lax.broadcasted_iota(jnp.int32, (CH, cols), 1)
    ones = jnp.ones((8, cols), F32)

    def turn(i, carry):
        for k in range(4):
            carry = turn_row(4 * i + k, *carry)
        return carry

    def turn_row(r, west, east):
        t = jnp.concatenate([fh[pl.ds(r, CH - 8, stride=rows), :], ones], axis=0)
        slab[r + 1, CH : 2 * CH, :] = t.astype(BF16)
        west = jnp.where(lane == r, jnp.broadcast_to(t[:, 0:1], (CH, cols)), west)
        east = jnp.where(lane == r, jnp.broadcast_to(t[:, cols - 1 : cols], (CH, cols)), east)
        return west, east

    zero = jnp.zeros((CH, cols), F32)
    west, east = lax.fori_loop(0, rows // 4, turn, (zero, zero))
    cols_out[0] = west.astype(BF16)
    cols_out[1] = east.astype(BF16)

    def rim(slot, src, dst, la, lo):
        return pltpu.make_async_remote_copy(
            src_ref=src, dst_ref=dst, send_sem=sh.at[slot], recv_sem=vh.at[slot],
            device_id=(la, lo), device_id_type=MESH,
        )

    to_south = [
        rim(0, slab.at[rows, pl.ds(CH, CH)], halo.at[0], south, b),
        rim(1, cols_out.at[1], cols_in.at[0, 0], south, right),
        rim(2, cols_out.at[0], cols_in.at[1, 0], south, left),
    ]
    to_north = [
        rim(3, slab.at[1, pl.ds(CH, CH)], halo.at[1], north, b),
        rim(4, cols_out.at[1], cols_in.at[0, 2], north, right),
        rim(5, cols_out.at[0], cols_in.at[1, 2], north, left),
    ]
    level = [
        rim(6, cols_out.at[1], cols_in.at[0, 1], a, right),
        rim(7, cols_out.at[0], cols_in.at[1, 1], a, left),
    ]
    for copy in level:
        copy.start()

    @pl.when(a < lats - 1)
    def _():
        for copy in to_south:
            copy.start()

    @pl.when(a > 0)
    def _():
        for copy in to_north:
            copy.start()

    load_trig.wait()
    loop(1, lons, lambda i: first(i).wait())
    lat_weight = weights_ref[pl.ds(group // packs, 1), :]
    circles = jnp.concatenate([r1[x] for x in range(lons)], axis=1)

    def member_block(ref, member):
        return ref.at[pl.ds(pl.multiple_of(member * block, block), block)]

    def zonal(member):
        at = pl.ds(pl.multiple_of(member * block, block), block)
        total = lax.dot_general(
            trig[at, :], circles, (((1,), (1,)), ((), ())), preferred_element_type=F32
        )
        return (total * lat_weight).astype(BF16)

    def second(i):
        peer = lax.rem(group + i, members)
        return pltpu.make_async_remote_copy(
            src_ref=member_block(fsend, peer), dst_ref=member_block(r2, group),
            send_sem=s2.at[i], recv_sem=v2.at[i],
            device_id=member_device(peer), device_id_type=MESH,
        )

    def zonal_send(i):
        peer = lax.rem(group + i, members)
        member_block(fsend, peer)[...] = zonal(peer)
        second(i).start()

    loop(1, members, zonal_send)
    member_block(r2, group)[...] = zonal(group)

    wide = 9 * CH
    spot = lax.broadcasted_iota(jnp.int32, (1, wide), 1)
    tap = spot // CH
    within = spot - tap * CH
    source = jnp.where(within < CH - 8, tap * (CH - 8) + within, -1)
    pick = lax.broadcasted_iota(jnp.int32, (gw_ref.shape[0], wide), 0) == source
    spread = lax.dot_general(
        gw_ref[...], jnp.where(pick, 1.0, 0.0).astype(BF16), (((0,), (0,)), ((), ())),
        preferred_element_type=F32,
    )
    bias = jnp.transpose(jnp.broadcast_to(bias_ref[...], (128, 256)))[:, 0:1]
    high = bias.astype(BF16).astype(F32)
    middle = (bias - high).astype(BF16).astype(F32)
    low = bias - high - middle
    base = 4 * CH + CH - 8
    spread += jnp.where(spot == base, high, 0.0)
    spread += jnp.where(spot == base + 1, middle, 0.0)
    spread += jnp.where(spot == base + 2, low, 0.0)
    gate_row = lax.broadcasted_iota(jnp.int32, (256, 1), 0) // 64
    gate_w[...] = (spread * jnp.where(gate_row == 2, 1.0, 0.5)).astype(BF16)

    for copy in level:
        copy.wait()

    @pl.when(a < lats - 1)
    def _():
        for copy in to_south:
            copy.wait_send()
        for copy in to_north:
            copy.wait_recv()

    @pl.when(a > 0)
    def _():
        for copy in to_north:
            copy.wait_send()
        for copy in to_south:
            copy.wait_recv()

    @pl.when(a == 0)
    def _():
        halo[0] = jnp.zeros((CH, cols), BF16)
        cols_in[0, 0] = jnp.zeros((CH, cols), BF16)
        cols_in[1, 0] = jnp.zeros((CH, cols), BF16)

    @pl.when(a == lats - 1)
    def _():
        halo[1] = jnp.zeros((CH, cols), BF16)
        cols_in[0, 2] = jnp.zeros((CH, cols), BF16)
        cols_in[1, 2] = jnp.zeros((CH, cols), BF16)

    def shifted(t, from_west, from_east, row):
        before = jnp.where(
            lane == 0, pltpu.roll(from_west, lax.rem(cols - row, cols), 1), pltpu.roll(t, 1, 1)
        )
        after = jnp.where(
            lane == cols - 1, pltpu.roll(from_east, cols - 1 - row, 1), pltpu.roll(t, cols - 1, 1)
        )
        return before.astype(BF16), after.astype(BF16)

    def keep(at, sides):
        slab[at, 0:CH, :] = sides[0]
        slab[at, 2 * CH : 3 * CH, :] = sides[1]

    def shift_rows(i):
        from_west, from_east = cols_in[0, 1].astype(F32), cols_in[1, 1].astype(F32)
        middle = [slab[4 * i + k + 1, CH : 2 * CH, :].astype(F32) for k in range(4)]
        sides = [shifted(middle[k], from_west, from_east, 4 * i + k) for k in range(4)]
        for k in range(4):
            keep(4 * i + k + 1, sides[k])

    loop(0, rows // 4, shift_rows)
    slab[0, CH : 2 * CH, :] = halo[0]
    slab[rows + 1, CH : 2 * CH, :] = halo[1]
    first_row, last_row = [
        shifted(halo[k].astype(F32), cols_in[0, 2 * k].astype(F32), cols_in[1, 2 * k].astype(F32), at)
        for k, at in ((0, rows - 1), (1, 0))
    ]
    keep(0, first_row)
    keep(rows + 1, last_row)

    load_leg.wait()
    loop(1, members, lambda i: second(i).wait())
    tiles = lats * rows // 128
    offsets = degree_offsets(members)
    share = len(offsets) - 1
    rates[...] = jnp.zeros_like(rates)
    rates[:, :KDEG] = relax_ref[...]
    rate_row = jnp.broadcast_to(rates[pl.ds(b // per_field, 1), :], (16, 512))
    rate_row = pltpu.roll(rate_row, lax.rem(512 - group, 512), 1)
    q_mode = lax.broadcasted_iota(jnp.int32, (16, 128), 0) // 2
    for u in range(block // 16):
        x = []
        for t in range(tiles):
            total = jnp.zeros((16, 128), F32)
            for g in range(t * packs, (t + 1) * packs):
                total += r2[g * block + 16 * u : g * block + 16 * (u + 1), :].astype(F32)
            x.append(total.astype(BF16))
        low, high = 8 * u, min(8 * (u + 1), share)
        basis = leg[offsets[low] : offsets[high], :]
        s = lax.dot_general(
            jnp.concatenate(x, axis=1), basis, (((1,), (1,)), ((), ())), preferred_element_type=F32
        )
        parts = []
        for i in range(low, high):
            rate = rate_row if i == 0 else pltpu.roll(rate_row, 512 - members * i, 1)
            if i == 0:
                rate = rate * jnp.where(group == 0, 1.0 / lon_total, 2.0 / lon_total)
            else:
                rate = rate * (2.0 / lon_total)
            for k in range(0, offsets[i + 1] - offsets[i], 128):
                at = offsets[i] - offsets[low] + k
                parts.append(
                    jnp.where(q_mode == i - low, s[:, at : at + 128] * rate[:, k : k + 128], 0.0)
                )
        nudged = jnp.concatenate(parts, axis=1).astype(BF16)
        y = jnp.dot(nudged, basis, preferred_element_type=F32).astype(BF16)
        for t in range(tiles):
            ysend[t, 16 * u : 16 * (u + 1), :] = y[:, t * 128 : (t + 1) * 128]

    def third(i):
        peer = lax.rem(group + i, members)
        return pltpu.make_async_remote_copy(
            src_ref=ysend.at[peer // packs], dst_ref=member_block(r3, group),
            send_sem=s3.at[i], recv_sem=v3.at[i],
            device_id=member_device(peer), device_id_type=MESH,
        )

    loop(1, members, lambda i: third(i).start())
    member_block(r3, group)[...] = ysend[group // packs]

    load_cell.wait()

    def pair(i):
        r = 2 * i
        patches = jnp.concatenate(
            [slab[pl.ds(r, 3)].reshape(wide, cols), slab[pl.ds(r + 1, 3)].reshape(wide, cols)], axis=1
        )
        g = jnp.tanh(jnp.dot(gate_w[...], patches, preferred_element_type=F32))
        old = jnp.concatenate(
            [cell[pl.ds(r, 64, stride=rows), :], cell[pl.ds(r + 1, 64, stride=rows), :]], axis=1
        )
        new = (0.5 * g[64:128] + 0.5) * old + (0.5 * g[0:64] + 0.5) * g[128:192]
        h = (0.5 * g[192:256] + 0.5) * jnp.tanh(new)
        cell_out[pl.ds(r, 64, stride=rows), :] = new[:, :cols]
        cell_out[pl.ds(r + 1, 64, stride=rows), :] = new[:, cols:]
        hid[pl.ds(r, 64, stride=rows), :] = h[:, :cols]
        hid[pl.ds(r + 1, 64, stride=rows), :] = h[:, cols:]
        inc = jnp.dot(ow_ref[...], h.astype(BF16), preferred_element_type=F32)
        pred[pl.ds(r, FIELDS, stride=rows), :] = inc[:, :cols]
        pred[pl.ds(r + 1, FIELDS, stride=rows), :] = inc[:, cols:]

    loop(0, rows // 4, pair)

    loop(1, members, lambda i: third(i).wait())
    turned[...] = jnp.transpose(r3[...].astype(F32)).astype(BF16)
    mine = turned[pl.ds(own_row, piece), :]

    def inverse(sector):
        at = pl.ds(pl.multiple_of(sector * cols, cols), cols)
        return jnp.dot(mine, trig[:, at], preferred_element_type=F32).astype(BF16)

    spot4 = pl.ds(pl.multiple_of(b * piece, piece), piece)

    def fourth(i):
        peer = lax.rem(b + i, lons)
        return lon_copy(i, csend.at[peer], r4.at[spot4], s4, v4)

    def inverse_send(i):
        peer = lax.rem(b + i, lons)
        csend[peer] = inverse(peer)
        fourth(i).start()

    loop(1, lons, inverse_send)
    r4[spot4, :] = inverse(b)

    loop(rows // 4, rows // 2, pair)

    def narrow(c):
        at = pl.ds(pl.multiple_of(c * 512, 512), 512)
        hidden_out[at, :] = hid[at, :].astype(BF16)

    loop(0, hidden_ref.shape[0] // 512, narrow)
    loop(1, lons, lambda i: fourth(i).wait())
    fields_out[...] = (
        fields_ref[...].astype(F32) + pred[...] + r4[...].astype(F32)
    ).astype(BF16)


def local(lats, lons, leg, trig, fields_in, hidden, cell_state, analysis, gate_weight, gate_bias, out_weight, relax_rates):
    hid, rows, cols = cell_state.shape
    lat_total = lats * rows
    piece = FIELDS * rows // lons
    members = lats * rows // piece
    quads = members * block_rows(members)
    phi = -0.5 * np.pi + (np.arange(lat_total) + 0.5) * np.pi / lat_total
    weights = (np.cos(phi) * np.pi / lat_total).astype(np.float32).reshape(-1, 128)
    vm = pl.BlockSpec(memory_space=pltpu.VMEM)
    hbm = pl.BlockSpec(memory_space=pl.ANY)
    n_rows = FIELDS * rows
    dma = pltpu.SemaphoreType.DMA
    out = pl.pallas_call(
        functools.partial(kernel, lats, lons, rows, cols),
        out_shape=(
            jax.ShapeDtypeStruct((n_rows, cols), BF16),
            jax.ShapeDtypeStruct((hid * rows, cols), BF16),
            jax.ShapeDtypeStruct((hid * rows, cols), F32),
        ),
        in_specs=[vm, vm, hbm, vm, vm, vm, vm, vm, vm, hbm, hbm],
        out_specs=(vm, vm, vm),
        scratch_shapes=[
            pltpu.VMEM((n_rows, cols), BF16),
            pltpu.VMEM((lons, 128, cols), BF16),
            pltpu.VMEM(((hid + FIELDS) * rows, cols), F32),
            pltpu.VMEM((rows + 2, 3 * CH, cols), BF16),
            pltpu.VMEM((2, CH, cols), BF16),
            pltpu.VMEM((2, CH, cols), BF16),
            pltpu.VMEM((2, 3, CH, cols), BF16),
            pltpu.VMEM((quads, 128), BF16),
            pltpu.VMEM((quads, 128), BF16),
            pltpu.VMEM((lat_total // 128, quads // members, 128), BF16),
            pltpu.VMEM((quads, 128), BF16),
            pltpu.VMEM((128, quads), BF16),
            pltpu.VMEM((lons, piece, cols), BF16),
            pltpu.VMEM((n_rows, cols), BF16),
            pltpu.VMEM((FIELDS, 512), F32),
            pltpu.VMEM((4 * hid, 9 * CH), BF16),
            pltpu.VMEM((n_rows, cols), F32),
            pltpu.VMEM((hid * rows, cols), F32),
            pltpu.VMEM(trig.shape, BF16),
            pltpu.VMEM(leg.shape[1:], BF16),
            pltpu.VMEM((hid * rows, cols), F32),
            dma((3,)),
            dma((lons,)), dma((lons,)), dma((members,)), dma((members,)),
            dma((members,)), dma((members,)), dma((lons,)), dma((lons,)),
            dma((8,)), dma((8,)),
        ],
        compiler_params=pltpu.CompilerParams(
            collective_id=0, has_side_effects=True, vmem_limit_bytes=56 * 1024 * 1024
        ),
    )(
        fields_in.reshape(n_rows, cols), hidden.reshape(hid * rows, cols),
        cell_state.reshape(hid * rows, cols), analysis.reshape(n_rows, cols),
        gate_weight.T, gate_bias.reshape(1, -1), out_weight, relax_rates, jnp.asarray(weights),
        jnp.asarray(trig), jnp.asarray(leg),
    )
    return (
        out[0].reshape(fields_in.shape), out[1].reshape(hidden.shape), out[2].reshape(cell_state.shape)
    )


def solution(mesh):
    lats, lons = mesh.shape["lat"], mesh.shape["lon"]

    def whole(*args):
        lat_total, lon_total = args[2].shape[1:]
        piece = FIELDS * (lat_total // lats) // lons
        leg = legendre_table(lat_total, lat_total // piece)
        trig = trig_table(lon_total, lat_total // piece)
        grid = P(None, "lat", "lon")
        return jax.shard_map(
            functools.partial(local, lats, lons, leg, trig),
            mesh=mesh,
            in_specs=(grid, grid, grid, grid, P(), P(), P(), P()),
            out_specs=(grid, grid, grid),
            check_vma=False,
        )(*args)

    return whole
```

```python
import functools
import math

import jax
import jax.numpy as jnp
import numpy as np
from jax import lax
from jax.experimental import pallas as pl
from jax.experimental.pallas import tpu as pltpu
from jax.sharding import PartitionSpec as P

FIELDS = 8
TRUNC = 213
MODES = 224
KDEG = 214
CH = 80
MESH = pl.DeviceIdType.MESH
F32 = jnp.float32
BF16 = jnp.bfloat16


def legendre_table(lat_total, members):
    order = np.arange(MODES) * 1.0
    ratios = np.ones(MODES)
    ratios[1:] = (2.0 * order[1:] + 1.0) / (2.0 * order[1:])
    diag_log = 0.5 * np.log(0.5) + np.cumsum(0.5 * np.log(ratios))
    phi = -0.5 * np.pi + (np.arange(lat_total) + 0.5) * np.pi / lat_total
    sine, cosine = np.sin(phi), np.cos(phi)
    table = np.zeros((KDEG, MODES, lat_total))
    table[0] = np.exp(diag_log[:, None] + order[:, None] * np.log(cosine)[None, :])
    table[1] = np.sqrt(2.0 * order + 3.0)[:, None] * sine[None, :] * table[0]
    for k in range(2, KDEG):
        n = order + k
        alpha = np.sqrt((4.0 * n**2 - 1.0) / (n**2 - order**2))
        beta = np.sqrt(((n - 1.0) ** 2 - order**2) / (4.0 * (n - 1.0) ** 2 - 1.0))
        table[k] = alpha[:, None] * (sine[None, :] * table[k - 1] - beta[:, None] * table[k - 2])
    degree = order[None, :] + np.arange(KDEG)[:, None]
    table *= (degree <= TRUNC)[:, :, None]
    offsets = degree_offsets(members)
    full = np.zeros((members, offsets[-1], lat_total))
    for member in range(members):
        for i, m in enumerate(range(member, MODES, members)):
            count = min(offsets[i + 1] - offsets[i], KDEG)
            full[member, offsets[i] : offsets[i] + count] = table[:count, m]
    return full.astype(np.float32).astype(BF16)


def degree_offsets(members):
    offsets = [0]
    for i in range(-(-MODES // members)):
        offsets.append(offsets[-1] + (256 if KDEG - members * i > 128 else 128))
    return offsets


def block_rows(members):
    return -(-2 * -(-MODES // members) // 16) * 16


def trig_table(lon_total, members):
    m = np.arange(-(-MODES // members) * members)
    phase = (m[:, None] * np.arange(lon_total)[None, :]) % lon_total
    angle = phase * (2.0 * np.pi / lon_total)
    both = np.stack([np.cos(angle), np.sin(angle)], axis=1) * (m <= TRUNC)[:, None, None]
    full = np.zeros((members, block_rows(members), lon_total))
    for member in range(members):
        part = both[member::members].reshape(-1, lon_total)
        full[member, : part.shape[0]] = part
    return full.reshape(-1, lon_total).astype(np.float32).astype(BF16)


def loop(start, stop, fn):
    def body(i, _):
        fn(i)
        return 0

    lax.fori_loop(start, stop, body, 0)


def kernel(
    lats, lons, rows, cols,
    fields_hbm, hidden_hbm, cell_hbm, analysis_hbm, gw_hbm, bias_hbm, ow_hbm, relax_hbm,
    weights_hbm, trig_hbm, leg_hbm,
    fields_out, hidden_out, cell_out,
    send1, r1, fh, slab, cols_out, halo, cols_in, fsend, r2, ysend, r3, turned, csend, r4, rates,
    gate_w, pred, hid, trig, leg, cell,
    fields_ref, hidden_ref, analysis_ref, gw_ref, bias_ref, ow_ref, relax_ref, weights_ref,
    load_sem, s1, v1, s2, v2, s3, v3, s4, v4, sh, vh,
):
    a, b = lax.axis_index("lat"), lax.axis_index("lon")
    piece = FIELDS * rows // lons
    per_field = rows // piece
    packs = 128 // piece
    group = a * per_field + lax.rem(b, per_field)
    members = lats * per_field
    block = block_rows(members)
    own_row = pl.multiple_of(lax.rem(group, packs) * piece, piece)
    lon_total = lons * cols

    def load(i, src, dst):
        copy = pltpu.make_async_copy(src, dst, load_sem.at[i])
        copy.start()
        return copy

    load_fields = load(0, fields_hbm, fields_ref)
    load_analysis = load(1, analysis_hbm, analysis_ref)
    load_hidden = load(2, hidden_hbm, hidden_ref)
    load_trig = load(3, trig_hbm, trig)
    load_weights = load(4, weights_hbm, weights_ref)
    load_gates = [load(5, gw_hbm, gw_ref), load(6, bias_hbm, bias_ref), load(7, ow_hbm, ow_ref)]
    load_relax = load(8, relax_hbm, relax_ref)
    load_leg = load(9, leg_hbm.at[group], leg)
    load_cell = load(10, cell_hbm, cell)

    r1[...] = jnp.zeros_like(r1)
    barrier = pltpu.get_barrier_semaphore()

    def member_device(member):
        return member // per_field, b - lax.rem(b, per_field) + lax.rem(member, per_field)

    def hello(la, lo):
        pl.semaphore_signal(barrier, inc=1, device_id=(la, lo), device_id_type=MESH)

    loop(1, lons, lambda i: hello(a, lax.rem(b + i, lons)))
    loop(1, members, lambda i: hello(*member_device(lax.rem(group + i, members))))
    left, right = lax.rem(b + lons - 1, lons), lax.rem(b + 1, lons)
    north, south = jnp.maximum(a - 1, 0), jnp.minimum(a + 1, lats - 1)

    @pl.when(a > 0)
    def _():
        hello(north, left)
        hello(north, right)

    @pl.when(a < lats - 1)
    def _():
        hello(south, left)
        hello(south, right)

    load_fields.wait()
    load_analysis.wait()
    send1[...] = (analysis_ref[...].astype(F32) - fields_ref[...].astype(F32)).astype(BF16)
    greeted = lons + members - 2
    greeted += 2 * (a > 0).astype(jnp.int32) + 2 * (a < lats - 1).astype(jnp.int32)
    pl.semaphore_wait(barrier, greeted)

    def lon_copy(i, src, dst, ssem, rsem):
        return pltpu.make_async_remote_copy(
            src_ref=src, dst_ref=dst, send_sem=ssem.at[i], recv_sem=rsem.at[i],
            device_id=(a, lax.rem(b + i, lons)), device_id_type=MESH,
        )

    def first(i):
        peer = lax.rem(b + i, lons)
        src = send1.at[pl.ds(pl.multiple_of(peer * piece, piece), piece)]
        return lon_copy(i, src, r1.at[b, pl.ds(own_row, piece)], s1, v1)

    loop(1, lons, lambda i: first(i).start())
    r1[b, pl.ds(own_row, piece), :] = send1[pl.ds(pl.multiple_of(b * piece, piece), piece), :]

    fh[0 : FIELDS * rows, :] = fields_ref[...].astype(F32)

    load_hidden.wait()

    def widen(c):
        at = pl.multiple_of(c * 512, 512)
        fh[pl.ds(pl.multiple_of(at + FIELDS * rows, 512), 512), :] = hidden_ref[
            pl.ds(at, 512), :
        ].astype(F32)

    loop(0, hidden_ref.shape[0] // 512, widen)
    lane = lax.broadcasted_iota(jnp.int32, (CH, cols), 1)
    ones = jnp.ones((8, cols), F32)

    def turn(i, carry):
        for k in range(4):
            carry = turn_row(4 * i + k, *carry)
        return carry

    def turn_row(r, west, east):
        t = jnp.concatenate([fh[pl.ds(r, CH - 8, stride=rows), :], ones], axis=0)
        slab[r + 1, CH : 2 * CH, :] = t.astype(BF16)
        west = jnp.where(lane == r, jnp.broadcast_to(t[:, 0:1], (CH, cols)), west)
        east = jnp.where(lane == r, jnp.broadcast_to(t[:, cols - 1 : cols], (CH, cols)), east)
        return west, east

    zero = jnp.zeros((CH, cols), F32)
    west, east = lax.fori_loop(0, rows // 4, turn, (zero, zero))
    cols_out[0] = west.astype(BF16)
    cols_out[1] = east.astype(BF16)

    def rim(slot, src, dst, la, lo):
        return pltpu.make_async_remote_copy(
            src_ref=src, dst_ref=dst, send_sem=sh.at[slot], recv_sem=vh.at[slot],
            device_id=(la, lo), device_id_type=MESH,
        )

    to_south = [
        rim(0, slab.at[rows, pl.ds(CH, CH)], halo.at[0], south, b),
        rim(1, cols_out.at[1], cols_in.at[0, 0], south, right),
        rim(2, cols_out.at[0], cols_in.at[1, 0], south, left),
    ]
    to_north = [
        rim(3, slab.at[1, pl.ds(CH, CH)], halo.at[1], north, b),
        rim(4, cols_out.at[1], cols_in.at[0, 2], north, right),
        rim(5, cols_out.at[0], cols_in.at[1, 2], north, left),
    ]
    level = [
        rim(6, cols_out.at[1], cols_in.at[0, 1], a, right),
        rim(7, cols_out.at[0], cols_in.at[1, 1], a, left),
    ]
    for copy in level:
        copy.start()

    @pl.when(a < lats - 1)
    def _():
        for copy in to_south:
            copy.start()

    @pl.when(a > 0)
    def _():
        for copy in to_north:
            copy.start()

    load_trig.wait()
    load_weights.wait()
    loop(1, lons, lambda i: first(i).wait())
    lat_weight = weights_ref[pl.ds(group // packs, 1), :]
    circles = jnp.concatenate([r1[x] for x in range(lons)], axis=1)

    def member_block(ref, member):
        return ref.at[pl.ds(pl.multiple_of(member * block, block), block)]

    def zonal(member):
        at = pl.ds(pl.multiple_of(member * block, block), block)
        total = lax.dot_general(
            trig[at, :], circles, (((1,), (1,)), ((), ())), preferred_element_type=F32
        )
        return (total * lat_weight).astype(BF16)

    def second(i):
        peer = lax.rem(group + i, members)
        return pltpu.make_async_remote_copy(
            src_ref=member_block(fsend, peer), dst_ref=member_block(r2, group),
            send_sem=s2.at[i], recv_sem=v2.at[i],
            device_id=member_device(peer), device_id_type=MESH,
        )

    def zonal_send(i):
        peer = lax.rem(group + i, members)
        member_block(fsend, peer)[...] = zonal(peer)
        second(i).start()

    loop(1, members, zonal_send)
    member_block(r2, group)[...] = zonal(group)

    for copy in load_gates:
        copy.wait()
    wide = 9 * CH
    spot = lax.broadcasted_iota(jnp.int32, (1, wide), 1)
    tap = spot // CH
    within = spot - tap * CH
    source = jnp.where(within < CH - 8, tap * (CH - 8) + within, -1)
    pick = lax.broadcasted_iota(jnp.int32, (gw_ref.shape[0], wide), 0) == source
    spread = lax.dot_general(
        gw_ref[...], jnp.where(pick, 1.0, 0.0).astype(BF16), (((0,), (0,)), ((), ())),
        preferred_element_type=F32,
    )
    bias = jnp.transpose(jnp.broadcast_to(bias_ref[...], (128, 256)))[:, 0:1]
    high = bias.astype(BF16).astype(F32)
    middle = (bias - high).astype(BF16).astype(F32)
    low = bias - high - middle
    base = 4 * CH + CH - 8
    spread += jnp.where(spot == base, high, 0.0)
    spread += jnp.where(spot == base + 1, middle, 0.0)
    spread += jnp.where(spot == base + 2, low, 0.0)
    gate_row = lax.broadcasted_iota(jnp.int32, (256, 1), 0) // 64
    gate_w[...] = (spread * jnp.where(gate_row == 2, 1.0, 0.5)).astype(BF16)

    for copy in level:
        copy.wait()

    @pl.when(a < lats - 1)
    def _():
        for copy in to_south:
            copy.wait_send()
        for copy in to_north:
            copy.wait_recv()

    @pl.when(a > 0)
    def _():
        for copy in to_north:
            copy.wait_send()
        for copy in to_south:
            copy.wait_recv()

    @pl.when(a == 0)
    def _():
        halo[0] = jnp.zeros((CH, cols), BF16)
        cols_in[0, 0] = jnp.zeros((CH, cols), BF16)
        cols_in[1, 0] = jnp.zeros((CH, cols), BF16)

    @pl.when(a == lats - 1)
    def _():
        halo[1] = jnp.zeros((CH, cols), BF16)
        cols_in[0, 2] = jnp.zeros((CH, cols), BF16)
        cols_in[1, 2] = jnp.zeros((CH, cols), BF16)

    def shifted(t, from_west, from_east, row):
        before = jnp.where(
            lane == 0, pltpu.roll(from_west, lax.rem(cols - row, cols), 1), pltpu.roll(t, 1, 1)
        )
        after = jnp.where(
            lane == cols - 1, pltpu.roll(from_east, cols - 1 - row, 1), pltpu.roll(t, cols - 1, 1)
        )
        return before.astype(BF16), after.astype(BF16)

    def keep(at, sides):
        slab[at, 0:CH, :] = sides[0]
        slab[at, 2 * CH : 3 * CH, :] = sides[1]

    def shift_rows(i):
        from_west, from_east = cols_in[0, 1].astype(F32), cols_in[1, 1].astype(F32)
        middle = [slab[4 * i + k + 1, CH : 2 * CH, :].astype(F32) for k in range(4)]
        sides = [shifted(middle[k], from_west, from_east, 4 * i + k) for k in range(4)]
        for k in range(4):
            keep(4 * i + k + 1, sides[k])

    loop(0, rows // 4, shift_rows)
    slab[0, CH : 2 * CH, :] = halo[0]
    slab[rows + 1, CH : 2 * CH, :] = halo[1]
    first_row, last_row = [
        shifted(halo[k].astype(F32), cols_in[0, 2 * k].astype(F32), cols_in[1, 2 * k].astype(F32), at)
        for k, at in ((0, rows - 1), (1, 0))
    ]
    keep(0, first_row)
    keep(rows + 1, last_row)

    load_leg.wait()
    load_relax.wait()
    loop(1, members, lambda i: second(i).wait())
    tiles = lats * rows // 128
    offsets = degree_offsets(members)
    share = len(offsets) - 1
    rates[...] = jnp.zeros_like(rates)
    rates[:, :KDEG] = relax_ref[...]
    rate_row = jnp.broadcast_to(rates[pl.ds(b // per_field, 1), :], (16, 512))
    rate_row = pltpu.roll(rate_row, lax.rem(512 - group, 512), 1)
    q_mode = lax.broadcasted_iota(jnp.int32, (16, 128), 0) // 2
    for u in range(block // 16):
        x = []
        for t in range(tiles):
            total = jnp.zeros((16, 128), F32)
            for g in range(t * packs, (t + 1) * packs):
                total += r2[g * block + 16 * u : g * block + 16 * (u + 1), :].astype(F32)
            x.append(total.astype(BF16))
        low, high = 8 * u, min(8 * (u + 1), share)
        basis = leg[offsets[low] : offsets[high], :]
        s = lax.dot_general(
            jnp.concatenate(x, axis=1), basis, (((1,), (1,)), ((), ())), preferred_element_type=F32
        )
        parts = []
        for i in range(low, high):
            rate = rate_row if i == 0 else pltpu.roll(rate_row, 512 - members * i, 1)
            if i == 0:
                rate = rate * jnp.where(group == 0, 1.0 / lon_total, 2.0 / lon_total)
            else:
                rate = rate * (2.0 / lon_total)
            for k in range(0, offsets[i + 1] - offsets[i], 128):
                at = offsets[i] - offsets[low] + k
                parts.append(
                    jnp.where(q_mode == i - low, s[:, at : at + 128] * rate[:, k : k + 128], 0.0)
                )
        nudged = jnp.concatenate(parts, axis=1).astype(BF16)
        y = jnp.dot(nudged, basis, preferred_element_type=F32).astype(BF16)
        for t in range(tiles):
            ysend[t, 16 * u : 16 * (u + 1), :] = y[:, t * 128 : (t + 1) * 128]

    def third(i):
        peer = lax.rem(group + i, members)
        return pltpu.make_async_remote_copy(
            src_ref=ysend.at[peer // packs], dst_ref=member_block(r3, group),
            send_sem=s3.at[i], recv_sem=v3.at[i],
            device_id=member_device(peer), device_id_type=MESH,
        )

    loop(1, members, lambda i: third(i).start())
    member_block(r3, group)[...] = ysend[group // packs]

    load_cell.wait()

    def pair(i):
        r = 2 * i
        patches = jnp.concatenate(
            [slab[pl.ds(r, 3)].reshape(wide, cols), slab[pl.ds(r + 1, 3)].reshape(wide, cols)], axis=1
        )
        g = jnp.tanh(jnp.dot(gate_w[...], patches, preferred_element_type=F32))
        old = jnp.concatenate(
            [cell[pl.ds(r, 64, stride=rows), :], cell[pl.ds(r + 1, 64, stride=rows), :]], axis=1
        )
        new = (0.5 * g[64:128] + 0.5) * old + (0.5 * g[0:64] + 0.5) * g[128:192]
        h = (0.5 * g[192:256] + 0.5) * jnp.tanh(new)
        cell_out[pl.ds(r, 64, stride=rows), :] = new[:, :cols]
        cell_out[pl.ds(r + 1, 64, stride=rows), :] = new[:, cols:]
        hid[pl.ds(r, 64, stride=rows), :] = h[:, :cols]
        hid[pl.ds(r + 1, 64, stride=rows), :] = h[:, cols:]
        inc = jnp.dot(ow_ref[...], h.astype(BF16), preferred_element_type=F32)
        pred[pl.ds(r, FIELDS, stride=rows), :] = inc[:, :cols]
        pred[pl.ds(r + 1, FIELDS, stride=rows), :] = inc[:, cols:]

    loop(0, rows // 4, pair)

    loop(1, members, lambda i: third(i).wait())
    turned[...] = jnp.transpose(r3[...].astype(F32)).astype(BF16)
    mine = turned[pl.ds(own_row, piece), :]

    def inverse(sector):
        at = pl.ds(pl.multiple_of(sector * cols, cols), cols)
        return jnp.dot(mine, trig[:, at], preferred_element_type=F32).astype(BF16)

    spot4 = pl.ds(pl.multiple_of(b * piece, piece), piece)

    def fourth(i):
        peer = lax.rem(b + i, lons)
        return lon_copy(i, csend.at[peer], r4.at[spot4], s4, v4)

    def inverse_send(i):
        peer = lax.rem(b + i, lons)
        csend[peer] = inverse(peer)
        fourth(i).start()

    loop(1, lons, inverse_send)
    r4[spot4, :] = inverse(b)

    loop(rows // 4, rows // 2, pair)

    def narrow(c):
        at = pl.ds(pl.multiple_of(c * 512, 512), 512)
        hidden_out[at, :] = hid[at, :].astype(BF16)

    loop(0, hidden_ref.shape[0] // 512, narrow)
    loop(1, lons, lambda i: fourth(i).wait())
    fields_out[...] = (
        fields_ref[...].astype(F32) + pred[...] + r4[...].astype(F32)
    ).astype(BF16)


def local(lats, lons, leg, trig, fields_in, hidden, cell_state, analysis, gate_weight, gate_bias, out_weight, relax_rates):
    hid, rows, cols = cell_state.shape
    lat_total = lats * rows
    piece = FIELDS * rows // lons
    members = lats * rows // piece
    quads = members * block_rows(members)
    phi = -0.5 * np.pi + (np.arange(lat_total) + 0.5) * np.pi / lat_total
    weights = (np.cos(phi) * np.pi / lat_total).astype(np.float32).reshape(-1, 128)
    vm = pl.BlockSpec(memory_space=pltpu.VMEM)
    hbm = pl.BlockSpec(memory_space=pl.ANY)
    n_rows = FIELDS * rows
    dma = pltpu.SemaphoreType.DMA
    out = pl.pallas_call(
        functools.partial(kernel, lats, lons, rows, cols),
        out_shape=(
            pltpu.VMEM((n_rows, cols), BF16),
            pltpu.VMEM((hid * rows, cols), BF16),
            pltpu.VMEM((hid * rows, cols), F32),
        ),
        in_specs=[hbm] * 11,
        out_specs=(vm, vm, vm),
        scratch_shapes=[
            pltpu.VMEM((n_rows, cols), BF16),
            pltpu.VMEM((lons, 128, cols), BF16),
            pltpu.VMEM(((hid + FIELDS) * rows, cols), F32),
            pltpu.VMEM((rows + 2, 3 * CH, cols), BF16),
            pltpu.VMEM((2, CH, cols), BF16),
            pltpu.VMEM((2, CH, cols), BF16),
            pltpu.VMEM((2, 3, CH, cols), BF16),
            pltpu.VMEM((quads, 128), BF16),
            pltpu.VMEM((quads, 128), BF16),
            pltpu.VMEM((lat_total // 128, quads // members, 128), BF16),
            pltpu.VMEM((quads, 128), BF16),
            pltpu.VMEM((128, quads), BF16),
            pltpu.VMEM((lons, piece, cols), BF16),
            pltpu.VMEM((n_rows, cols), BF16),
            pltpu.VMEM((FIELDS, 512), F32),
            pltpu.VMEM((4 * hid, 9 * CH), BF16),
            pltpu.VMEM((n_rows, cols), F32),
            pltpu.VMEM((hid * rows, cols), F32),
            pltpu.VMEM(trig.shape, BF16),
            pltpu.VMEM(leg.shape[1:], BF16),
            pltpu.VMEM((hid * rows, cols), F32),
            pltpu.VMEM((n_rows, cols), BF16),
            pltpu.VMEM((hid * rows, cols), BF16),
            pltpu.VMEM((n_rows, cols), BF16),
            pltpu.VMEM(gate_weight.shape[::-1], BF16),
            pltpu.VMEM((1, 4 * hid), F32),
            pltpu.VMEM(out_weight.shape, BF16),
            pltpu.VMEM(relax_rates.shape, F32),
            pltpu.VMEM(weights.shape, F32),
            dma((11,)),
            dma((lons,)), dma((lons,)), dma((members,)), dma((members,)),
            dma((members,)), dma((members,)), dma((lons,)), dma((lons,)),
            dma((8,)), dma((8,)),
        ],
        compiler_params=pltpu.CompilerParams(
            collective_id=0, has_side_effects=True, vmem_limit_bytes=60 * 1024 * 1024
        ),
    )(
        fields_in.reshape(n_rows, cols), hidden.reshape(hid * rows, cols),
        cell_state.reshape(hid * rows, cols), analysis.reshape(n_rows, cols),
        gate_weight.T, gate_bias.reshape(1, -1), out_weight, relax_rates, jnp.asarray(weights),
        jnp.asarray(trig), jnp.asarray(leg),
    )
    return (
        out[0].reshape(fields_in.shape), out[1].reshape(hidden.shape), out[2].reshape(cell_state.shape)
    )


def solution(mesh):
    lats, lons = mesh.shape["lat"], mesh.shape["lon"]

    def whole(*args):
        lat_total, lon_total = args[2].shape[1:]
        piece = FIELDS * (lat_total // lats) // lons
        leg = legendre_table(lat_total, lat_total // piece)
        trig = trig_table(lon_total, lat_total // piece)
        grid = P(None, "lat", "lon")
        return jax.shard_map(
            functools.partial(local, lats, lons, leg, trig),
            mesh=mesh,
            in_specs=(grid, grid, grid, grid, P(), P(), P(), P()),
            out_specs=(grid, grid, grid),
            check_vma=False,
        )(*args)

    return whole
```
